32 devices in a mesh: ty: 8 (over z, y), tx: 4 (over x, core).
Axes of the slice: x: 2, y: 2, z: 4, core: 2. Of those that a mesh axis runs over, the one named last changes fastest.
Arguments:
- object_slices: float32 [2, 2, 4096, 2048], P(None, None, 'ty', 'tx'), may hold values from -1.1 to 1.1
- probe: float32 [2, 256, 256], replicated, may hold values from -4.2 to 4.2
- fresnel_phase: float32 [256, 256], replicated, may hold values from -3.140625 to 3.140625
- intensity: float32 [8, 4, 4, 256, 256], P('ty', 'tx'), may hold values from 0.05 to 2
- offsets: int32 [8, 4, 4, 2], P('ty', 'tx'), may hold values from -128 to 384, as said below
- counts: int32 [8, 4], replicated, may hold values from 1 to 4, as said below
Outputs:
- new_object: float32 [2, 2, 4096, 2048], P(None, None, 'ty', 'tx')
The draws below stay inside these ranges and needn't reach their ends.
Inputs may be any that keep to these rules, and one draw needn't show every extreme that they name: The positions of a tile fill its slots 0 to counts - 1; some tile has 4. `offsets`: every window of 256 x 256 pixels lies inside the object.
All inputs are finite; a program needn't handle non-finite values.
Results may differ from the reference program's by a relative error of at most 0.0003.
Values sent between devices are 32-bit elements; how exact they have to be, the bound alone decides.
A program may use at most 128 MiB of HBM per device.

```python
import math
import jax
import jax.numpy as jnp
from jax import lax

PATCH = 256
TILE = 512
SLICES = 2
CAP = 4
HALF = 128
GRID_Y = 8
GRID_X = 4
NPY = 4096
NPX = 2048


def draw_object_slices(key, part):
    key_amp, key_phase = jax.random.split(key)
    shape = (SLICES, NPY, NPX)
    amplitude = jax.random.uniform(key_amp, shape, jnp.float32, 0.6, 1.0)
    phase = jax.random.uniform(key_phase, shape, jnp.float32, -1.0, 1.0)
    return jnp.stack([amplitude * jnp.cos(phase), amplitude * jnp.sin(phase)], axis=1).astype(jnp.float32)


def draw_offsets(key, part):
    key_raw, key_y, key_x = jax.random.split(jax.random.fold_in(key, 11), 3)
    raw = jax.random.randint(key_raw, (GRID_Y, GRID_X, CAP, 2), -HALF, TILE - HALF + 1)
    tile_rows = jnp.arange(GRID_Y, dtype=jnp.int32)[:, None, None]
    tile_cols = jnp.arange(GRID_X, dtype=jnp.int32)[None, :, None]
    slot_index = jnp.arange(CAP, dtype=jnp.int32)[None, None, :]
    rows = jnp.clip(tile_rows * TILE + raw[..., 0], 0, GRID_Y * TILE - PATCH) - tile_rows * TILE
    cols = jnp.clip(tile_cols * TILE + raw[..., 1], 0, GRID_X * TILE - PATCH) - tile_cols * TILE
    pick_y = jax.random.randint(key_y, (), 1, GRID_Y - 1)
    pick_x = jax.random.randint(key_x, (), 1, GRID_X - 1)
    chosen = (tile_rows == pick_y) & (tile_cols == pick_x)
    rows = jnp.where(chosen & (slot_index == 0), -HALF, rows)
    rows = jnp.where(chosen & (slot_index == 1), TILE - HALF, rows)
    cols = jnp.where(chosen & (slot_index == 0), -HALF, cols)
    cols = jnp.where(chosen & (slot_index == 1), TILE - HALF, cols)
    return jnp.stack([rows, cols], axis=-1).astype(jnp.int32)


def draw_counts(key, part):
    key_base, key_y, key_x = jax.random.split(jax.random.fold_in(key, 23), 3)
    base = jax.random.randint(key_base, (GRID_Y, GRID_X), 1, 3)
    centre_y = jax.random.randint(key_y, (), 0, GRID_Y - 2)
    centre_x = jax.random.randint(key_x, (), 0, GRID_X // 2 - 1)
    rows = jnp.arange(GRID_Y, dtype=jnp.int32)[:, None]
    cols = jnp.arange(GRID_X, dtype=jnp.int32)[None, :]
    dense = (rows >= centre_y) & (rows <= centre_y + 2) & (cols >= centre_x) & (cols <= centre_x + 1)
    return jnp.where(dense, CAP, base).astype(jnp.int32)


def level_of(own_key, extent, pieces, low, largest):
    def one(position, parts):
        draws = jax.random.uniform(jax.random.fold_in(jax.random.fold_in(own_key, 6), position), (parts,), jnp.float32, low / len(pieces), largest / len(pieces))
        return jnp.repeat(jnp.exp(draws), extent[position] // parts).reshape((-1,) + (1,) * (len(extent) - position - 1))

    loudness = one(*pieces[0])
    for cut in pieces[1:]:
        loudness = loudness * one(*cut)
    return loudness


def centred(key, shape, width, bound, kind=jnp.bfloat16):
    result = jax.random.normal(key, shape, jnp.float32) * width
    return jnp.minimum(jnp.maximum(result, -bound), bound).astype(kind)


def setup_inputs(seed: int = 0) -> dict:
    splits = jax.random.split(jax.random.key(seed), 7)
    return {
        "object_slices": draw_object_slices(jax.random.fold_in(splits[6], 71), 0),
        "probe": centred(splits[1], (2, PATCH, PATCH), 0.7, 4.2, jnp.float32),
        "fresnel_phase": jnp.clip(jax.random.uniform(splits[2], (PATCH, PATCH), jnp.float32, -3.140625, 3.140625), -3.140625, 3.140625),
        "intensity": jnp.clip(jnp.exp(math.log(2.0) - 3.6888794 * jax.random.uniform(splits[3], (GRID_Y, GRID_X, CAP, PATCH, PATCH), jnp.float32) ** level_of(splits[3], (GRID_Y, GRID_X, CAP, PATCH, PATCH), ((0, 8), (1, 4)), -0.2, 0.2)), 0.05, 2.0),
        "offsets": draw_offsets(jax.random.fold_in(splits[6], 71), 0),
        "counts": draw_counts(jax.random.fold_in(splits[6], 71), 0),
    }


HIGH = lax.Precision.HIGHEST
STEP_SIZE = 0.25

def dft_basis(length):
    index = jnp.arange(length, dtype=jnp.int32)
    turns = index[:, None] * index[None, :] % length
    angles = turns.astype(jnp.float32) * (2.0 * math.pi / length)
    scale = 1.0 / math.sqrt(length)
    return (jnp.cos(angles) * scale, -jnp.sin(angles) * scale)

def matmul_high(left, right):
    return jnp.dot(left, right, precision=HIGH, preferred_element_type=jnp.float32)

def complex_matmul(left_re, left_im, right_re, right_im):
    real = matmul_high(left_re, right_re) - matmul_high(left_im, right_im)
    imag = matmul_high(left_re, right_im) + matmul_high(left_im, right_re)
    return (real, imag)

def forward_dft(field_re, field_im, basis_re, basis_im):
    temp_re, temp_im = complex_matmul(basis_re, basis_im, field_re, field_im)
    return complex_matmul(temp_re, temp_im, basis_re, basis_im)

def complex_times(left_re, left_im, right_re, right_im):
    return (left_re * right_re - left_im * right_im, left_re * right_im + left_im * right_re)

def conj_times(left_re, left_im, right_re, right_im):
    return (left_re * right_re + left_im * right_im, left_im * right_re - left_re * right_im)

def position_grad(window, measured, probe, kernel_re, kernel_im, basis_re, basis_im):
    first_re, first_im = complex_times(probe[0], probe[1], window[0, 0], window[0, 1])
    spec_re, spec_im = forward_dft(first_re, first_im, basis_re, basis_im)
    spec_re, spec_im = complex_times(kernel_re, kernel_im, spec_re, spec_im)
    phi_re, phi_im = forward_dft(spec_re, spec_im, basis_re, -basis_im)
    exit_re, exit_im = complex_times(phi_re, phi_im, window[1, 0], window[1, 1])
    far_re, far_im = forward_dft(exit_re, exit_im, basis_re, basis_im)
    misfit = far_re * far_re + far_im * far_im - measured
    back_re, back_im = forward_dft(misfit * far_re, misfit * far_im, basis_re, -basis_im)
    second_re, second_im = conj_times(back_re, back_im, phi_re, phi_im)
    wave_re, wave_im = conj_times(back_re, back_im, window[1, 0], window[1, 1])
    wave_re, wave_im = forward_dft(wave_re, wave_im, basis_re, basis_im)
    wave_re, wave_im = conj_times(wave_re, wave_im, kernel_re, kernel_im)
    wave_re, wave_im = forward_dft(wave_re, wave_im, basis_re, -basis_im)
    lead_re, lead_im = conj_times(wave_re, wave_im, probe[0], probe[1])
    return jnp.stack([jnp.stack([lead_re, lead_im]), jnp.stack([second_re, second_im])])

def reference(object_slices, probe, fresnel_phase, intensity, offsets, counts):
    basis_re, basis_im = dft_basis(PATCH)
    kernel_re = jnp.cos(fresnel_phase)
    kernel_im = jnp.sin(fresnel_phase)
    total = GRID_Y * GRID_X * CAP
    zero_index = jnp.zeros((), jnp.int32)

    def one_position(gradient, number):
        tile_y = number // (GRID_X * CAP)
        tile_x = number // CAP % GRID_X
        slot = number % CAP
        row = (tile_y * TILE + offsets[tile_y, tile_x, slot, 0]).astype(jnp.int32)
        column = (tile_x * TILE + offsets[tile_y, tile_x, slot, 1]).astype(jnp.int32)
        live = (slot < counts[tile_y, tile_x]).astype(jnp.float32)
        start = (zero_index, zero_index, row, column)
        window = lax.dynamic_slice(object_slices, start, (SLICES, 2, PATCH, PATCH))
        term = position_grad(window, intensity[tile_y, tile_x, slot], probe, kernel_re, kernel_im, basis_re, basis_im) * live
        current = lax.dynamic_slice(gradient, start, (SLICES, 2, PATCH, PATCH))
        return (lax.dynamic_update_slice(gradient, current + term, start), None)
    gradient, unused = lax.scan(one_position, jnp.zeros_like(object_slices), jnp.arange(total, dtype=jnp.int32))
    return object_slices - STEP_SIZE * gradient
```

```python
import functools
import math

import jax
import jax.numpy as jnp
import ml_dtypes
import numpy as np
from jax import lax
from jax.experimental import pallas as pl
from jax.experimental.pallas import tpu as pltpu
from jax.sharding import PartitionSpec as P

STEP_SIZE = 0.25
F32 = jnp.float32
BF16 = jnp.bfloat16


def passed_along(value, axis, steps):
    count = lax.axis_size(axis)
    first, last = (max(0, -steps), min(count, count - steps))
    return lax.ppermute(value, axis, [(source, source + steps) for source in range(first, last)])


def basis_blocks(length):
    half = length // 2
    index = np.arange(length)
    turns = (index[:, None] * index[None, :]) % length
    angles = turns * (2.0 * math.pi / length)
    real = np.cos(angles) / math.sqrt(length)
    imag = -np.sin(angles) / math.sqrt(length)
    forms = []
    for parity in (0, 1):
        c_re, c_im = real[:half, parity::2], imag[:half, parity::2]
        forms.append(np.block([[c_re, c_im], [-c_im, c_re]]))
    forms = np.stack([forms[0], forms[1], forms[0].T, forms[1].T]).astype(np.float32)
    high = forms.astype(ml_dtypes.bfloat16)
    low = (forms - high.astype(np.float32)).astype(ml_dtypes.bfloat16)
    return np.stack([high, low], axis=1)


def parted(value):
    high = value.astype(BF16)
    return high, (value - high.astype(F32)).astype(BF16)


def dot(left, right):
    return jnp.dot(left, right, preferred_element_type=F32)


def on_lanes(value, w, which):
    high, low = parted(value)
    return dot(high, w[which, 0]) + dot(low, w[which, 0]) + dot(high, w[which, 1])


def on_rows(value, w, which):
    high, low = parted(value)
    return dot(w[which, 0], high) + dot(w[which, 0], low) + dot(w[which, 1], high)


def cut(value, axis):
    half = value.shape[axis] // 2
    return (value[:half], value[half:]) if axis == 0 else (value[:, :half], value[:, half:])


def forward(re, im, w):
    for axis, apply, base in ((0, on_rows, 2), (1, on_lanes, 0)):
        re_a, re_b = cut(re, axis)
        im_a, im_b = cut(im, axis)
        even = apply(jnp.concatenate([re_a + re_b, im_a + im_b], axis), w, base)
        odd = apply(jnp.concatenate([re_a - re_b, im_a - im_b], axis), w, base + 1)
        even_re, even_im = cut(even, axis)
        odd_re, odd_im = cut(odd, axis)
        re = jnp.concatenate([even_re, odd_re], axis)
        im = jnp.concatenate([even_im, odd_im], axis)
    return re, im


def backward(re, im, w):
    for axis, apply, base in ((0, on_rows, 0), (1, on_lanes, 2)):
        re_a, re_b = cut(re, axis)
        im_a, im_b = cut(im, axis)
        even = apply(jnp.concatenate([re_a, im_a], axis), w, base)
        odd = apply(jnp.concatenate([re_b, im_b], axis), w, base + 1)
        sum_re, sum_im = cut(even + odd, axis)
        dif_re, dif_im = cut(even - odd, axis)
        re = jnp.concatenate([sum_re, dif_re], axis)
        im = jnp.concatenate([sum_im, dif_im], axis)
    return re, im


def complex_times(left_re, left_im, right_re, right_im):
    return (left_re * right_re - left_im * right_im, left_re * right_im + left_im * right_re)


def conj_times(left_re, left_im, right_re, right_im):
    return (left_re * right_re + left_im * right_im, left_im * right_re - left_re * right_im)


def gather_padded(layer, obj, up, down, left, right, cor_left, cor_right, pad, sem):
    half = up.shape[1]
    tile = obj.shape[-1]
    end = half + tile
    mid, first, last = pl.ds(half, tile), pl.ds(0, half), pl.ds(end, half)
    pairs = [
        (obj.at[layer], pad.at[:, mid, mid]),
        (up, pad.at[:, first, mid]),
        (down, pad.at[:, last, mid]),
        (left.at[layer], pad.at[:, mid, first]),
        (right.at[layer], pad.at[:, mid, last]),
        (cor_left.at[0], pad.at[:, first, first]),
        (cor_left.at[1], pad.at[:, last, first]),
        (cor_right.at[0], pad.at[:, first, last]),
        (cor_right.at[1], pad.at[:, last, last]),
    ]
    copies = [pltpu.make_async_copy(a, b, sem.at[i]) for i, (a, b) in enumerate(pairs)]
    for copy in copies:
        copy.start()
    for copy in copies:
        copy.wait()


def corner(places, slot, patch):
    y, x = places[slot, 0], places[slot, 1]
    row = pl.multiple_of(y // 8 * 8, 8)
    lane = pl.multiple_of(x // 128 * 128, 128)
    return pl.ds(row, patch + 8), pl.ds(lane, patch + 128), y % 8, x % 128


def window(pad, places, slot, patch):
    rows, lanes, down, along = corner(places, slot, patch)
    tall, wide = patch + 8, patch + 128
    found = []
    for c in range(2):
        value = pltpu.roll(pad[c, rows, lanes], (wide - along) % wide, 1)[:, :patch]
        found.append(pltpu.roll(value, (tall - down) % tall, 0)[:patch])
    return found


def add_window(total, places, slot, terms):
    patch = terms[0].shape[0]
    rows, lanes, down, along = corner(places, slot, patch)
    for c in range(2):
        value = jnp.concatenate([terms[c], jnp.zeros((8, patch), F32)], 0)
        value = pltpu.roll(value, down, 0)
        value = jnp.concatenate([value, jnp.zeros((patch + 8, 128), F32)], 1)
        total[c, rows, lanes] += pltpu.roll(value, along, 1)


def write_pieces(total, out_left, out_mid, out_right):
    half = out_left.shape[-1]
    tile = out_mid.shape[-1]
    rows = out_mid.shape[1]
    out_left[...] = total[:, :rows, :half]
    out_mid[...] = total[:, :rows, half : half + tile]
    out_right[...] = total[:, :rows, half + tile : 2 * half + tile]


def first_kernel(mine, places, obj, up, down, left, right, cl, cr, probe, prop, w, phi, pad, sem):
    patch = probe.shape[-1]
    gather_padded(0, obj, up, down, left, right, cl, cr, pad, sem)

    def step(slot, carry):
        o_re, o_im = window(pad, places, slot, patch)
        re, im = complex_times(probe[0], probe[1], o_re, o_im)
        re, im = forward(re, im, w)
        re, im = complex_times(prop[0], prop[1], re, im)
        re, im = backward(re, im, w)
        phi[slot, 0] = re
        phi[slot, 1] = im
        return carry

    lax.fori_loop(0, mine[0], step, 0)


def second_kernel(
    mine, places, obj, up, down, left, right, cl, cr, phi, measured, w,
    wave, out_left, out_mid, out_right, pad, total, sem,
):
    patch = phi.shape[-1]
    gather_padded(1, obj, up, down, left, right, cl, cr, pad, sem)
    total[...] = jnp.zeros_like(total)

    def step(slot, carry):
        o_re, o_im = window(pad, places, slot, patch)
        re, im = complex_times(phi[slot, 0], phi[slot, 1], o_re, o_im)
        re, im = forward(re, im, w)
        misfit = re * re + im * im - measured[slot]
        re, im = backward(misfit * re, misfit * im, w)
        add_window(total, places, slot, conj_times(re, im, phi[slot, 0], phi[slot, 1]))
        o_re, o_im = window(pad, places, slot, patch)
        re, im = conj_times(re, im, o_re, o_im)
        wave[slot, 0] = re
        wave[slot, 1] = im
        return carry

    lax.fori_loop(0, mine[0], step, 0)
    write_pieces(total, out_left, out_mid, out_right)


def third_kernel(mine, places, wave, probe, prop, w, out_left, out_mid, out_right, total):
    total[...] = jnp.zeros_like(total)

    def step(slot, carry):
        re, im = forward(wave[slot, 0], wave[slot, 1], w)
        re, im = conj_times(re, im, prop[0], prop[1])
        re, im = backward(re, im, w)
        add_window(total, places, slot, conj_times(re, im, probe[0], probe[1]))
        return carry

    lax.fori_loop(0, mine[0], step, 0)
    write_pieces(total, out_left, out_mid, out_right)


def evens_first(array):
    for axis in (-2, -1):
        array = jnp.concatenate(
            [lax.slice_in_dim(array, s, array.shape[axis], stride=2, axis=axis) for s in (0, 1)],
            axis=axis,
        )
    return array


def spread(piece, before, after, axis):
    pads = [(0, 0)] * piece.ndim
    pads[axis] = (before, after)
    return jnp.pad(piece, pads)


def shards(object_slices, probe, fresnel_phase, intensity, offsets, counts):
    patch = probe.shape[-1]
    half = patch // 2
    tile = object_slices.shape[-1]
    slots = intensity.shape[2]
    long = tile + 2 * half
    smem = pl.BlockSpec(memory_space=pltpu.SMEM)
    vmem = pl.BlockSpec(memory_space=pltpu.VMEM)
    anym = pl.BlockSpec(memory_space=pl.ANY)
    params = pltpu.CompilerParams(vmem_limit_bytes=48 * 2**20)
    wide_scratch = pltpu.VMEM((2, long + 8, long + 128), F32)
    waves = jax.ShapeDtypeStruct((slots, 2, patch, patch), F32)
    pieces = [
        jax.ShapeDtypeStruct((2, long, half), F32),
        jax.ShapeDtypeStruct((2, long, tile), F32),
        jax.ShapeDtypeStruct((2, long, half), F32),
    ]
    cost = pl.CostEstimate(flops=8 * 10**9, bytes_accessed=10**7, transcendentals=0)

    w = jnp.asarray(basis_blocks(patch))
    first, last = object_slices[:, :, :half], object_slices[:, :, tile - half :]
    up1 = passed_along(last[0], "ty", 1)
    down1 = passed_along(first[0], "ty", -1)
    left = passed_along(object_slices[:, :, :, tile - half :], "tx", 1)
    right = passed_along(object_slices[:, :, :, :half], "tx", -1)
    last2, first2, up1, down1 = lax.optimization_barrier((last[1], first[1], up1, down1))
    up2 = passed_along(last2, "ty", 1)
    down2 = passed_along(first2, "ty", -1)

    def corners(up, down):
        ends = jnp.stack([up[:, :, tile - half :], down[:, :, tile - half :]])
        starts = jnp.stack([up[:, :, :half], down[:, :, :half]])
        return passed_along(ends, "tx", 1), passed_along(starts, "tx", -1)

    prop_phase = evens_first(fresnel_phase)
    prop = jnp.stack([jnp.cos(prop_phase), jnp.sin(prop_phase)])
    measured = evens_first(intensity[0, 0])
    places = offsets[0, 0] + half
    mine = counts[lax.axis_index("ty"), lax.axis_index("tx")].reshape(1)

    phi = pl.pallas_call(
        first_kernel,
        out_shape=waves,
        in_specs=[smem] * 2 + [anym] * 7 + [vmem] * 3,
        out_specs=vmem,
        scratch_shapes=[wide_scratch, pltpu.SemaphoreType.DMA((9,))],
        compiler_params=params,
        cost_estimate=cost,
    )(mine, places, object_slices, up1, down1, left, right, *corners(up1, down1), probe, prop, w)

    wave, left2, mid2, right2 = pl.pallas_call(
        second_kernel,
        out_shape=[waves] + pieces,
        in_specs=[smem] * 2 + [anym] * 7 + [vmem] * 3,
        out_specs=[vmem] * 4,
        scratch_shapes=[wide_scratch, wide_scratch, pltpu.SemaphoreType.DMA((9,))],
        compiler_params=params,
        cost_estimate=cost,
    )(mine, places, object_slices, up2, down2, left, right, *corners(up2, down2), phi, measured, w)

    def third(wave):
        return pl.pallas_call(
            third_kernel,
            out_shape=pieces,
            in_specs=[smem] * 2 + [vmem] * 4,
            out_specs=[vmem] * 3,
            scratch_shapes=[wide_scratch],
            compiler_params=params,
            cost_estimate=cost,
        )(mine, places, wave, probe, prop, w)

    def columns_in(left, mid, right):
        return passed_along(right, "tx", 1), passed_along(left, "tx", -1)

    def rows_of(mid, before, after, start, size):
        part = lax.slice_in_dim(mid, start, start + size, axis=1)
        part = part + spread(before[:, start : start + size], 0, tile - half, 2)
        return part + spread(after[:, start : start + size], tile - half, 0, 2)

    def rows_in(mid, before, after):
        top = rows_of(mid, before, after, 0, half)
        bottom = rows_of(mid, before, after, half + tile, half)
        return passed_along(bottom, "ty", 1), passed_along(top, "ty", -1)

    def core(mid, before, after, above, below):
        whole = rows_of(mid, before, after, half, tile)
        return whole + spread(above, 0, tile - half, 1) + spread(below, tile - half, 0, 1)

    before2, after2 = columns_in(left2, mid2, right2)
    left1, mid1, right1 = third(wave)
    above2, below2 = rows_in(mid2, before2, after2)
    before1, after1 = columns_in(left1, mid1, right1)
    above1, below1 = rows_in(mid1, before1, after1)
    total = jnp.stack(
        [core(mid1, before1, after1, above1, below1), core(mid2, before2, after2, above2, below2)]
    )
    return object_slices - STEP_SIZE * total


def solution(mesh):
    placed = (
        P(None, None, "ty", "tx"),
        P(),
        P(),
        P("ty", "tx", None, None, None),
        P("ty", "tx", None, None),
        P(),
    )
    return jax.shard_map(
        shards, mesh=mesh, in_specs=placed, out_specs=P(None, None, "ty", "tx"), check_vma=False
    )
```

```python
import functools
import math

import jax
import jax.numpy as jnp
import ml_dtypes
import numpy as np
from jax import lax
from jax.experimental import pallas as pl
from jax.experimental.pallas import tpu as pltpu
from jax.sharding import PartitionSpec as P

STEP_SIZE = 0.25
F32 = jnp.float32
BF16 = jnp.bfloat16


def passed_along(value, axis, steps):
    count = lax.axis_size(axis)
    first, last = (max(0, -steps), min(count, count - steps))
    return lax.ppermute(value, axis, [(source, source + steps) for source in range(first, last)])


def basis_blocks(length):
    half = length // 2
    index = np.arange(length)
    turns = (index[:, None] * index[None, :]) % length
    angles = turns * (2.0 * math.pi / length)
    real = np.cos(angles) / math.sqrt(length)
    imag = -np.sin(angles) / math.sqrt(length)
    forms = []
    for parity in (0, 1):
        c_re, c_im = real[:half, parity::2], imag[:half, parity::2]
        forms.append(np.block([[c_re, c_im], [-c_im, c_re]]))
    forms = np.stack([forms[0], forms[1], forms[0].T, forms[1].T]).astype(np.float32)
    high = forms.astype(ml_dtypes.bfloat16)
    low = (forms - high.astype(np.float32)).astype(ml_dtypes.bfloat16)
    return np.concatenate([high, high, low], axis=1), np.concatenate([high, high, low], axis=2)


def order_matrix(length):
    order = np.concatenate([np.arange(0, length, 2), np.arange(1, length, 2)])
    matrix = np.zeros((length, length), ml_dtypes.bfloat16)
    matrix[order, np.arange(length)] = 1
    return np.stack([matrix, matrix.T])


def parted(value):
    high = value.astype(BF16)
    return high, (value - high.astype(F32)).astype(BF16)


def dot(left, right):
    return jnp.dot(left, right, preferred_element_type=F32)


def on_lanes(value, w, which):
    high, low = parted(value)
    return dot(jnp.concatenate([high, low, high], 1), w[0][which])


def on_rows(value, w, which):
    high, low = parted(value)
    return dot(w[1][which], jnp.concatenate([high, low, high], 0))


def cut(value, axis):
    half = value.shape[axis] // 2
    return (value[:half], value[half:]) if axis == 0 else (value[:, :half], value[:, half:])


def forward(re, im, w):
    for axis, apply, base in ((0, on_rows, 2), (1, on_lanes, 0)):
        re_a, re_b = cut(re, axis)
        im_a, im_b = cut(im, axis)
        even = apply(jnp.concatenate([re_a + re_b, im_a + im_b], axis), w, base)
        odd = apply(jnp.concatenate([re_a - re_b, im_a - im_b], axis), w, base + 1)
        even_re, even_im = cut(even, axis)
        odd_re, odd_im = cut(odd, axis)
        re = jnp.concatenate([even_re, odd_re], axis)
        im = jnp.concatenate([even_im, odd_im], axis)
    return re, im


def backward(re, im, w):
    for axis, apply, base in ((0, on_rows, 0), (1, on_lanes, 2)):
        re_a, re_b = cut(re, axis)
        im_a, im_b = cut(im, axis)
        even = apply(jnp.concatenate([re_a, im_a], axis), w, base)
        odd = apply(jnp.concatenate([re_b, im_b], axis), w, base + 1)
        sum_re, sum_im = cut(even + odd, axis)
        dif_re, dif_im = cut(even - odd, axis)
        re = jnp.concatenate([sum_re, dif_re], axis)
        im = jnp.concatenate([sum_im, dif_im], axis)
    return re, im


def complex_times(left_re, left_im, right_re, right_im):
    return (left_re * right_re - left_im * right_im, left_re * right_im + left_im * right_re)


def conj_times(left_re, left_im, right_re, right_im):
    return (left_re * right_re + left_im * right_im, left_im * right_re - left_re * right_im)


def gather_padded(layer, obj, up, down, left, right, cor_left, cor_right, pad, sem):
    half = up.shape[1]
    tile = obj.shape[-1]
    end = half + tile
    mid, first, last = pl.ds(half, tile), pl.ds(0, half), pl.ds(end, half)
    pairs = [
        (obj.at[layer], pad.at[:, mid, mid]),
        (up, pad.at[:, first, mid]),
        (down, pad.at[:, last, mid]),
        (left.at[layer], pad.at[:, mid, first]),
        (right.at[layer], pad.at[:, mid, last]),
        (cor_left.at[0], pad.at[:, first, first]),
        (cor_left.at[1], pad.at[:, last, first]),
        (cor_right.at[0], pad.at[:, first, last]),
        (cor_right.at[1], pad.at[:, last, last]),
    ]
    copies = [pltpu.make_async_copy(a, b, sem.at[i]) for i, (a, b) in enumerate(pairs)]
    for copy in copies:
        copy.start()
    for copy in copies:
        copy.wait()


def corner(places, slot, patch):
    y, x = places[slot, 0], places[slot, 1]
    row = pl.multiple_of(y // 8 * 8, 8)
    lane = pl.multiple_of(x // 128 * 128, 128)
    return pl.ds(row, patch + 8), pl.ds(lane, patch + 128), y % 8, x % 128


def window(pad, places, slot, patch):
    rows, lanes, down, along = corner(places, slot, patch)
    tall, wide = patch + 8, patch + 128
    found = []
    for c in range(2):
        value = pltpu.roll(pad[c, rows, lanes], (wide - along) % wide, 1)[:, :patch]
        found.append(pltpu.roll(value, (tall - down) % tall, 0)[:patch])
    return found


def add_window(total, places, slot, terms):
    patch = terms[0].shape[0]
    rows, lanes, down, along = corner(places, slot, patch)
    for c in range(2):
        value = jnp.concatenate([terms[c], jnp.zeros((8, patch), F32)], 0)
        value = pltpu.roll(value, down, 0)
        value = jnp.concatenate([value, jnp.zeros((patch + 8, 128), F32)], 1)
        total[c, rows, lanes] += pltpu.roll(value, along, 1)


def write_pieces(total, out_left, out_mid, out_right, out_top, out_bottom):
    half = out_left.shape[-1]
    tile = out_mid.shape[-1]
    rows = out_mid.shape[1]
    out_left[...] = total[:, :rows, :half]
    out_mid[...] = total[:, :rows, half : half + tile]
    out_right[...] = total[:, :rows, half + tile : 2 * half + tile]
    out_top[...] = total[:, :half, 2 * half : tile]
    out_bottom[...] = total[:, half + tile : 2 * half + tile, 2 * half : tile]


def order_kernel(measured, waves, order, out_measured, out_waves):
    def ordered(value):
        for axis in (0, 1):
            high, low = parted(value)
            least = (value - high.astype(F32) - low.astype(F32)).astype(BF16)
            if axis == 0:
                high, low, least = [dot(order[1], part) for part in (high, low, least)]
            else:
                high, low, least = [dot(part, order[0]) for part in (high, low, least)]
            value = high + (low + least)
        return value

    def step(slot, carry):
        out_measured[slot] = ordered(measured[slot])
        return carry

    lax.fori_loop(0, measured.shape[0], step, 0)
    out_waves[0] = ordered(waves[0])
    out_waves[1] = ordered(waves[1])


def first_kernel(
    mine, places, obj, up, down, left, right, cl, cr, probe, prop, w0, w1, phi, pad, sem
):
    w = (w0, w1)
    patch = probe.shape[-1]
    gather_padded(0, obj, up, down, left, right, cl, cr, pad, sem)

    def step(slot, carry):
        o_re, o_im = window(pad, places, slot, patch)
        re, im = complex_times(probe[0], probe[1], o_re, o_im)
        re, im = forward(re, im, w)
        re, im = complex_times(prop[0], prop[1], re, im)
        re, im = backward(re, im, w)
        phi[slot, 0] = re
        phi[slot, 1] = im
        return carry

    lax.fori_loop(0, mine[0], step, 0)


def second_kernel(
    mine, places, obj, up, down, left, right, cl, cr, phi, measured, w0, w1,
    wave, out_left, out_mid, out_right, out_top, out_bottom, pad, total, sem,
):
    w = (w0, w1)
    patch = phi.shape[-1]
    gather_padded(1, obj, up, down, left, right, cl, cr, pad, sem)
    total[...] = jnp.zeros_like(total)

    def step(slot, carry):
        o_re, o_im = window(pad, places, slot, patch)
        re, im = complex_times(phi[slot, 0], phi[slot, 1], o_re, o_im)
        re, im = forward(re, im, w)
        misfit = re * re + im * im - measured[slot]
        re, im = backward(misfit * re, misfit * im, w)
        add_window(total, places, slot, conj_times(re, im, phi[slot, 0], phi[slot, 1]))
        o_re, o_im = window(pad, places, slot, patch)
        re, im = conj_times(re, im, o_re, o_im)
        wave[slot, 0] = re
        wave[slot, 1] = im
        return carry

    lax.fori_loop(0, mine[0], step, 0)
    write_pieces(total, out_left, out_mid, out_right, out_top, out_bottom)


def third_kernel(
    mine, places, wave, probe, prop, w0, w1,
    out_left, out_mid, out_right, out_top, out_bottom, total,
):
    w = (w0, w1)
    total[...] = jnp.zeros_like(total)

    def step(slot, carry):
        re, im = forward(wave[slot, 0], wave[slot, 1], w)
        re, im = conj_times(re, im, prop[0], prop[1])
        re, im = backward(re, im, w)
        add_window(total, places, slot, conj_times(re, im, probe[0], probe[1]))
        return carry

    lax.fori_loop(0, mine[0], step, 0)
    write_pieces(total, out_left, out_mid, out_right, out_top, out_bottom)


def spread(piece, before, after, axis):
    pads = [(0, 0)] * piece.ndim
    pads[axis] = (before, after)
    return jnp.pad(piece, pads)


def shards(object_slices, probe, fresnel_phase, intensity, offsets, counts):
    patch = probe.shape[-1]
    half = patch // 2
    tile = object_slices.shape[-1]
    slots = intensity.shape[2]
    long = tile + 2 * half
    smem = pl.BlockSpec(memory_space=pltpu.SMEM)
    vmem = pl.BlockSpec(memory_space=pltpu.VMEM)
    anym = pl.BlockSpec(memory_space=pl.ANY)
    params = pltpu.CompilerParams(vmem_limit_bytes=48 * 2**20)
    wide_scratch = pltpu.VMEM((2, long + 8, long + 128), F32)
    waves = jax.ShapeDtypeStruct((slots, 2, patch, patch), F32)
    pieces = [
        jax.ShapeDtypeStruct((2, long, half), F32),
        jax.ShapeDtypeStruct((2, long, tile), F32),
        jax.ShapeDtypeStruct((2, long, half), F32),
        jax.ShapeDtypeStruct((2, half, tile - 2 * half), F32),
        jax.ShapeDtypeStruct((2, half, tile - 2 * half), F32),
    ]
    cost = pl.CostEstimate(flops=8 * 10**9, bytes_accessed=10**7, transcendentals=0)

    w0, w1 = [jnp.asarray(form) for form in basis_blocks(patch)]
    first, last = object_slices[:, :, :half], object_slices[:, :, tile - half :]
    up1 = passed_along(last[0], "ty", 1)
    down1 = passed_along(first[0], "ty", -1)
    left = passed_along(object_slices[:, :, :, tile - half :], "tx", 1)
    right = passed_along(object_slices[:, :, :, :half], "tx", -1)
    def corners(up, down):
        ends = jnp.stack([up[:, :, tile - half :], down[:, :, tile - half :]])
        starts = jnp.stack([up[:, :, :half], down[:, :, :half]])
        return passed_along(ends, "tx", 1), passed_along(starts, "tx", -1)

    measured, prop = pl.pallas_call(
        order_kernel,
        out_shape=[
            jax.ShapeDtypeStruct((slots, patch, patch), F32),
            jax.ShapeDtypeStruct((2, patch, patch), F32),
        ],
        in_specs=[vmem] * 3,
        out_specs=[vmem] * 2,
        compiler_params=params,
        cost_estimate=cost,
    )(
        intensity[0, 0],
        jnp.stack([jnp.cos(fresnel_phase), jnp.sin(fresnel_phase)]),
        jnp.asarray(order_matrix(patch)),
    )
    last2, first2, up1, down1, measured, prop = lax.optimization_barrier(
        (last[1], first[1], up1, down1, measured, prop)
    )
    up2 = passed_along(last2, "ty", 1)
    down2 = passed_along(first2, "ty", -1)
    places = offsets[0, 0] + half
    mine = counts[lax.axis_index("ty"), lax.axis_index("tx")].reshape(1)

    phi = pl.pallas_call(
        first_kernel,
        out_shape=waves,
        in_specs=[smem] * 2 + [anym] * 7 + [vmem] * 4,
        out_specs=vmem,
        scratch_shapes=[wide_scratch, pltpu.SemaphoreType.DMA((9,))],
        compiler_params=params,
        cost_estimate=cost,
    )(mine, places, object_slices, up1, down1, left, right, *corners(up1, down1), probe, prop, w0, w1)

    up2, down2, phi = lax.optimization_barrier((up2, down2, phi))
    wave, *pieces2 = pl.pallas_call(
        second_kernel,
        out_shape=[waves] + pieces,
        in_specs=[smem] * 2 + [anym] * 7 + [vmem] * 4,
        out_specs=[vmem] * 6,
        scratch_shapes=[wide_scratch, wide_scratch, pltpu.SemaphoreType.DMA((9,))],
        compiler_params=params,
        cost_estimate=cost,
    )(mine, places, object_slices, up2, down2, left, right, *corners(up2, down2), phi, measured, w0, w1)

    def third(wave):
        return pl.pallas_call(
            third_kernel,
            out_shape=pieces,
            in_specs=[smem] * 2 + [vmem] * 5,
            out_specs=[vmem] * 5,
            scratch_shapes=[wide_scratch],
            compiler_params=params,
            cost_estimate=cost,
        )(mine, places, wave, probe, prop, w0, w1)

    def columns_in(left, right):
        return passed_along(right, "tx", 1), passed_along(left, "tx", -1)

    def rows_in(top, bottom):
        return passed_along(bottom, "ty", 1), passed_along(top, "ty", -1)

    def edges_of(mid, before, after, start):
        rows = slice(start, start + half)
        starts = mid[:, rows, :half] + before[:, rows]
        ends = mid[:, rows, tile - half :] + after[:, rows]
        return jnp.concatenate([starts, ends], axis=2)

    def core(mid, before, after, above, below, edge_above, edge_below):
        whole = mid[:, half : half + tile]
        whole = whole + spread(before[:, half : half + tile], 0, tile - half, 2)
        whole = whole + spread(after[:, half : half + tile], tile - half, 0, 2)

        def joined(middle, edge):
            return jnp.concatenate([edge[:, :, :half], middle, edge[:, :, half:]], axis=2)

        whole = whole + spread(joined(above, edge_above), 0, tile - half, 1)
        return whole + spread(joined(below, edge_below), tile - half, 0, 1)

    left2, mid2, right2, top2, bottom2 = pieces2
    above2, below2 = rows_in(top2, bottom2)
    before2, after2 = columns_in(left2, right2)
    left1, mid1, right1, top1, bottom1 = third(wave)
    above1, below1 = rows_in(top1, bottom1)
    left1, right1, above2, below2 = lax.optimization_barrier((left1, right1, above2, below2))
    before1, after1 = columns_in(left1, right1)

    def both_edges(start):
        return jnp.stack(
            [edges_of(mid1, before1, after1, start), edges_of(mid2, before2, after2, start)]
        )

    tops, bottoms, above1, below1 = lax.optimization_barrier(
        (both_edges(0), both_edges(half + tile), above1, below1)
    )
    edges_above, edges_below = rows_in(tops, bottoms)
    total = jnp.stack(
        [
            core(mid1, before1, after1, above1, below1, edges_above[0], edges_below[0]),
            core(mid2, before2, after2, above2, below2, edges_above[1], edges_below[1]),
        ]
    )
    return object_slices - STEP_SIZE * total


def solution(mesh):
    placed = (
        P(None, None, "ty", "tx"),
        P(),
        P(),
        P("ty", "tx", None, None, None),
        P("ty", "tx", None, None),
        P(),
    )
    return jax.shard_map(
        shards, mesh=mesh, in_specs=placed, out_specs=P(None, None, "ty", "tx"), check_vma=False
    )
```

```python
import functools
import math

import jax
import jax.numpy as jnp
import ml_dtypes
import numpy as np
from jax import lax
from jax.experimental import pallas as pl
from jax.experimental.pallas import tpu as pltpu
from jax.sharding import PartitionSpec as P

STEP_SIZE = 0.25
F32 = jnp.float32
BF16 = jnp.bfloat16


def passed_along(value, axis, steps):
    count = lax.axis_size(axis)
    first, last = (max(0, -steps), min(count, count - steps))
    return lax.ppermute(value, axis, [(source, source + steps) for source in range(first, last)])


def basis_blocks(length):
    half = length // 2
    index = np.arange(length)
    turns = (index[:, None] * index[None, :]) % length
    angles = turns * (2.0 * math.pi / length)
    real = np.cos(angles) / math.sqrt(length)
    imag = -np.sin(angles) / math.sqrt(length)
    forms = []
    for parity in (0, 1):
        c_re, c_im = real[:half, parity::2], imag[:half, parity::2]
        forms.append(np.block([[c_re, c_im], [-c_im, c_re]]))
    forms = np.stack([forms[0], forms[1], forms[0].T, forms[1].T]).astype(np.float32)
    high = forms.astype(ml_dtypes.bfloat16)
    low = (forms - high.astype(np.float32)).astype(ml_dtypes.bfloat16)
    return np.concatenate([high, high, low], axis=1), np.concatenate([high, high, low], axis=2)


def order_matrix(length):
    order = np.concatenate([np.arange(0, length, 2), np.arange(1, length, 2)])
    matrix = np.zeros((length, length), ml_dtypes.bfloat16)
    matrix[order, np.arange(length)] = 1
    return np.stack([matrix, matrix.T])


def parted(value):
    high = value.astype(BF16)
    return high, (value - high.astype(F32)).astype(BF16)


def dot(left, right):
    return jnp.dot(left, right, preferred_element_type=F32)


def on_lanes(value, w, which):
    high, low = parted(value)
    return dot(jnp.concatenate([high, low, high], 1), w[0][which])


def on_rows(value, w, which):
    high, low = parted(value)
    return dot(w[1][which], jnp.concatenate([high, low, high], 0))


def cut(value, axis):
    half = value.shape[axis] // 2
    return (value[:half], value[half:]) if axis == 0 else (value[:, :half], value[:, half:])


def forward(re, im, w):
    for axis, apply, base in ((0, on_rows, 2), (1, on_lanes, 0)):
        re_a, re_b = cut(re, axis)
        im_a, im_b = cut(im, axis)
        even = apply(jnp.concatenate([re_a + re_b, im_a + im_b], axis), w, base)
        odd = apply(jnp.concatenate([re_a - re_b, im_a - im_b], axis), w, base + 1)
        even_re, even_im = cut(even, axis)
        odd_re, odd_im = cut(odd, axis)
        re = jnp.concatenate([even_re, odd_re], axis)
        im = jnp.concatenate([even_im, odd_im], axis)
    return re, im


def backward(re, im, w):
    for axis, apply, base in ((0, on_rows, 0), (1, on_lanes, 2)):
        re_a, re_b = cut(re, axis)
        im_a, im_b = cut(im, axis)
        even = apply(jnp.concatenate([re_a, im_a], axis), w, base)
        odd = apply(jnp.concatenate([re_b, im_b], axis), w, base + 1)
        sum_re, sum_im = cut(even + odd, axis)
        dif_re, dif_im = cut(even - odd, axis)
        re = jnp.concatenate([sum_re, dif_re], axis)
        im = jnp.concatenate([sum_im, dif_im], axis)
    return re, im


def complex_times(left_re, left_im, right_re, right_im):
    return (left_re * right_re - left_im * right_im, left_re * right_im + left_im * right_re)


def conj_times(left_re, left_im, right_re, right_im):
    return (left_re * right_re + left_im * right_im, left_im * right_re - left_re * right_im)


def gather_padded(layer, obj, rows, left, right, cor_left, cor_right, pad, sem):
    half = left.shape[-1]
    tile = obj.shape[-1]
    end = half + tile
    mid, first, last = pl.ds(half, tile), pl.ds(0, half), pl.ds(end, half)
    pairs = [
        (obj.at[layer], pad.at[:, mid, mid]),
        (left.at[layer], pad.at[:, mid, first]),
        (right.at[layer], pad.at[:, mid, last]),
    ]
    for side, there in ((0, first), (1, last)):
        pairs.append((cor_left.at[layer, side], pad.at[:, there, first]))
        pairs.append((cor_right.at[layer, side], pad.at[:, there, last]))
        if len(rows) == 2:
            pairs.append((rows[side], pad.at[:, there, mid]))
        else:
            edge, inner = rows[side], rows[2 + side]
            pairs.append((edge.at[:, :, pl.ds(0, half)], pad.at[:, there, pl.ds(half, half)]))
            pairs.append((edge.at[:, :, pl.ds(half, half)], pad.at[:, there, pl.ds(tile, half)]))
            pairs.append((inner, pad.at[:, there, pl.ds(2 * half, tile - 2 * half)]))
    copies = [pltpu.make_async_copy(a, b, sem.at[i]) for i, (a, b) in enumerate(pairs)]
    for copy in copies:
        copy.start()
    for copy in copies:
        copy.wait()


def corner(places, slot, patch):
    y, x = places[slot, 0], places[slot, 1]
    row = pl.multiple_of(y // 8 * 8, 8)
    lane = pl.multiple_of(x // 128 * 128, 128)
    return pl.ds(row, patch + 8), pl.ds(lane, patch + 128), y % 8, x % 128


def window(pad, places, slot, patch):
    rows, lanes, down, along = corner(places, slot, patch)
    tall, wide = patch + 8, patch + 128
    found = []
    for c in range(2):
        value = pltpu.roll(pad[c, rows, lanes], (wide - along) % wide, 1)[:, :patch]
        found.append(pltpu.roll(value, (tall - down) % tall, 0)[:patch])
    return found


def add_window(total, places, slot, terms):
    patch = terms[0].shape[0]
    rows, lanes, down, along = corner(places, slot, patch)
    for c in range(2):
        value = jnp.concatenate([terms[c], jnp.zeros((8, patch), F32)], 0)
        value = pltpu.roll(value, down, 0)
        value = jnp.concatenate([value, jnp.zeros((patch + 8, 128), F32)], 1)
        total[c, rows, lanes] += pltpu.roll(value, along, 1)


def write_pieces(total, out_mid, out_top, out_bottom):
    half = out_top.shape[1]
    tile = out_mid.shape[-1]
    rows = out_mid.shape[1]
    out_mid[...] = total[:, :rows, half : half + tile]
    out_top[...] = total[:, :half, 2 * half : tile]
    out_bottom[...] = total[:, half + tile : 2 * half + tile, 2 * half : tile]


def write_sides(total, corners, sides):
    half = sides[0].shape[-1]
    tile = sides[0].shape[1]
    for out_corner, out_side, start in zip(corners, sides, (0, half + tile)):
        lanes = slice(start, start + half)
        out_corner[0] = total[:, :half, lanes]
        out_corner[1] = total[:, half + tile : 2 * half + tile, lanes]
        out_side[...] = total[:, half : half + tile, lanes]


def order_kernel(measured, waves, order, out_measured, out_waves):
    def ordered(value):
        for axis in (0, 1):
            high, low = parted(value)
            least = (value - high.astype(F32) - low.astype(F32)).astype(BF16)
            if axis == 0:
                high, low, least = [dot(order[1], part) for part in (high, low, least)]
            else:
                high, low, least = [dot(part, order[0]) for part in (high, low, least)]
            value = high + (low + least)
        return value

    def step(slot, carry):
        out_measured[slot] = ordered(measured[slot])
        return carry

    lax.fori_loop(0, measured.shape[0], step, 0)
    out_waves[0] = ordered(waves[0])
    out_waves[1] = ordered(waves[1])


def first_kernel(
    mine, places, obj, up, down, left, right, cl, cr, probe, prop, w0, w1, phi, pad, sem
):
    w = (w0, w1)
    patch = probe.shape[-1]
    gather_padded(0, obj, (up, down), left, right, cl, cr, pad, sem)

    def step(slot, carry):
        o_re, o_im = window(pad, places, slot, patch)
        re, im = complex_times(probe[0], probe[1], o_re, o_im)
        re, im = forward(re, im, w)
        re, im = complex_times(prop[0], prop[1], re, im)
        re, im = backward(re, im, w)
        phi[slot, 0] = re
        phi[slot, 1] = im
        return carry

    lax.fori_loop(0, mine[0], step, 0)


def second_kernel(
    mine, places, obj, up, down, up_mid, down_mid, left, right, cl, cr, phi, measured, w0, w1,
    wave, out_mid, out_top, out_bottom, out_cl, out_cr, out_left, out_right, pad, total, sem,
):
    w = (w0, w1)
    patch = phi.shape[-1]
    gather_padded(1, obj, (up, down, up_mid, down_mid), left, right, cl, cr, pad, sem)
    total[...] = jnp.zeros_like(total)

    def step(slot, carry):
        o_re, o_im = window(pad, places, slot, patch)
        re, im = complex_times(phi[slot, 0], phi[slot, 1], o_re, o_im)
        re, im = forward(re, im, w)
        misfit = re * re + im * im - measured[slot]
        re, im = backward(misfit * re, misfit * im, w)
        add_window(total, places, slot, conj_times(re, im, phi[slot, 0], phi[slot, 1]))
        o_re, o_im = window(pad, places, slot, patch)
        re, im = conj_times(re, im, o_re, o_im)
        wave[slot, 0] = re
        wave[slot, 1] = im
        return carry

    lax.fori_loop(0, mine[0], step, 0)
    write_pieces(total, out_mid, out_top, out_bottom)
    write_sides(total, (out_cl, out_cr), (out_left, out_right))


def third_kernel(
    mine, places, wave, probe, prop, w0, w1, cl, cr, left, right,
    out_mid, out_top, out_bottom, out_cl, out_cr, out_left, out_right, total,
):
    w = (w0, w1)
    total[...] = jnp.zeros_like(total)

    def step(slot, carry):
        re, im = forward(wave[slot, 0], wave[slot, 1], w)
        re, im = conj_times(re, im, prop[0], prop[1])
        re, im = backward(re, im, w)
        add_window(total, places, slot, conj_times(re, im, probe[0], probe[1]))
        return carry

    lax.fori_loop(0, mine[0], step, 0)
    write_pieces(total, out_mid, out_top, out_bottom)
    write_sides(
        total, (out_cl.at[0], out_cr.at[0]), (out_left.at[0], out_right.at[0])
    )
    for out, value in ((out_cl, cl), (out_cr, cr), (out_left, left), (out_right, right)):
        out[1] = value[...]


def spread(piece, before, after, axis):
    pads = [(0, 0)] * piece.ndim
    pads[axis] = (before, after)
    return jnp.pad(piece, pads)


def shards(object_slices, probe, fresnel_phase, intensity, offsets, counts):
    patch = probe.shape[-1]
    half = patch // 2
    tile = object_slices.shape[-1]
    slots = intensity.shape[2]
    long = tile + 2 * half
    smem = pl.BlockSpec(memory_space=pltpu.SMEM)
    vmem = pl.BlockSpec(memory_space=pltpu.VMEM)
    anym = pl.BlockSpec(memory_space=pl.ANY)
    params = pltpu.CompilerParams(vmem_limit_bytes=48 * 2**20)
    wide_scratch = pltpu.VMEM((2, long + 8, long + 128), F32)
    waves = jax.ShapeDtypeStruct((slots, 2, patch, patch), F32)
    pieces = [
        jax.ShapeDtypeStruct((2, long, tile), F32),
        jax.ShapeDtypeStruct((2, half, tile - 2 * half), F32),
        jax.ShapeDtypeStruct((2, half, tile - 2 * half), F32),
    ]
    side_shapes = [(2, 2, half, half)] * 2 + [(2, tile, half)] * 2
    sides = [jax.ShapeDtypeStruct(shape, F32) for shape in side_shapes]
    both_sides = [jax.ShapeDtypeStruct((2,) + shape, F32) for shape in side_shapes]
    cost = pl.CostEstimate(flops=8 * 10**9, bytes_accessed=10**7, transcendentals=0)

    w0, w1 = [jnp.asarray(form) for form in basis_blocks(patch)]
    first, last = object_slices[:, :, :half], object_slices[:, :, tile - half :]
    up1 = passed_along(last[0], "ty", 1)
    down1 = passed_along(first[0], "ty", -1)


    def outer(piece):
        return jnp.concatenate([piece[:, :, :half], piece[:, :, tile - half :]], axis=2)

    def inner(piece):
        return piece[:, :, half : tile - half]

    up2 = passed_along(outer(last[1]), "ty", 1)
    down2 = passed_along(outer(first[1]), "ty", -1)
    left = passed_along(object_slices[:, :, :, tile - half :], "tx", 1)
    right = passed_along(object_slices[:, :, :, :half], "tx", -1)
    measured, prop = pl.pallas_call(
        order_kernel,
        out_shape=[
            jax.ShapeDtypeStruct((slots, patch, patch), F32),
            jax.ShapeDtypeStruct((2, patch, patch), F32),
        ],
        in_specs=[vmem] * 3,
        out_specs=[vmem] * 2,
        compiler_params=params,
        cost_estimate=cost,
    )(
        intensity[0, 0],
        jnp.stack([jnp.cos(fresnel_phase), jnp.sin(fresnel_phase)]),
        jnp.asarray(order_matrix(patch)),
    )
    last2, first2, up1, down1, measured, prop = lax.optimization_barrier(
        (inner(last[1]), inner(first[1]), up1, down1, measured, prop)
    )
    up2_mid = passed_along(last2, "ty", 1)
    down2_mid = passed_along(first2, "ty", -1)

    def corners(up, down, up_next, down_next):
        return jnp.stack([jnp.stack([up, down]), jnp.stack([up_next, down_next])])

    ends = corners(
        up1[:, :, tile - half :], down1[:, :, tile - half :], up2[:, :, half:], down2[:, :, half:]
    )
    starts = corners(up1[:, :, :half], down1[:, :, :half], up2[:, :, :half], down2[:, :, :half])
    halo = (left, right, passed_along(ends, "tx", 1), passed_along(starts, "tx", -1))
    places = offsets[0, 0] + half
    mine = counts[lax.axis_index("ty"), lax.axis_index("tx")].reshape(1)

    phi = pl.pallas_call(
        first_kernel,
        out_shape=waves,
        in_specs=[smem] * 2 + [anym] * 7 + [vmem] * 4,
        out_specs=vmem,
        scratch_shapes=[wide_scratch, pltpu.SemaphoreType.DMA((13,))],
        compiler_params=params,
        cost_estimate=cost,
    )(mine, places, object_slices, up1, down1, *halo, probe, prop, w0, w1)

    up2_mid, down2_mid, phi = lax.optimization_barrier((up2_mid, down2_mid, phi))
    wave, *pieces2 = pl.pallas_call(
        second_kernel,
        out_shape=[waves] + pieces + sides,
        in_specs=[smem] * 2 + [anym] * 9 + [vmem] * 4,
        out_specs=[vmem] * 8,
        scratch_shapes=[wide_scratch, wide_scratch, pltpu.SemaphoreType.DMA((13,))],
        compiler_params=params,
        cost_estimate=cost,
    )(
        mine, places, object_slices, up2, down2, up2_mid, down2_mid, *halo, phi, measured, w0, w1
    )

    def third(wave, *sides2):
        return pl.pallas_call(
            third_kernel,
            out_shape=pieces + both_sides,
            in_specs=[smem] * 2 + [vmem] * 9,
            out_specs=[vmem] * 7,
            scratch_shapes=[wide_scratch],
            compiler_params=params,
            cost_estimate=cost,
        )(mine, places, wave, probe, prop, w0, w1, *sides2)

    def columns_in(left, right):
        return passed_along(right, "tx", 1), passed_along(left, "tx", -1)

    def rows_in(top, bottom):
        return passed_along(bottom, "ty", 1), passed_along(top, "ty", -1)

    def edges_of(mid, before, after, start):
        rows = slice(start, start + half)
        starts = mid[:, rows, :half] + before
        ends = mid[:, rows, tile - half :] + after
        return jnp.concatenate([starts, ends], axis=2)

    def core(mid, before, after, above, below, edge_above, edge_below):
        whole = mid[:, half : half + tile]
        whole = whole + spread(before, 0, tile - half, 2)
        whole = whole + spread(after, tile - half, 0, 2)

        def joined(middle, edge):
            return jnp.concatenate([edge[:, :, :half], middle, edge[:, :, half:]], axis=2)

        whole = whole + spread(joined(above, edge_above), 0, tile - half, 1)
        return whole + spread(joined(below, edge_below), tile - half, 0, 1)

    mid2, top2, bottom2, *sides2 = pieces2
    above2, below2 = rows_in(top2, bottom2)
    mid1, top1, bottom1, cor_left, cor_right, side_left, side_right = third(wave, *sides2)
    cor_left, cor_right, above2, below2 = lax.optimization_barrier(
        (cor_left, cor_right, above2, below2)
    )
    above1, below1 = rows_in(top1, bottom1)
    cor_before, cor_after = columns_in(cor_left, cor_right)

    def both_edges(side):
        start = side * (half + tile)
        return jnp.stack(
            [
                edges_of(mid1, cor_before[0, side], cor_after[0, side], start),
                edges_of(mid2, cor_before[1, side], cor_after[1, side], start),
            ]
        )

    tops, bottoms, above1, below1, side_left, side_right = lax.optimization_barrier(
        (both_edges(0), both_edges(1), above1, below1, side_left, side_right)
    )
    edges_above, edges_below = rows_in(tops, bottoms)
    before, after = columns_in(side_left, side_right)
    total = jnp.stack(
        [
            core(mid1, before[0], after[0], above1, below1, edges_above[0], edges_below[0]),
            core(mid2, before[1], after[1], above2, below2, edges_above[1], edges_below[1]),
        ]
    )
    return object_slices - STEP_SIZE * total


def solution(mesh):
    placed = (
        P(None, None, "ty", "tx"),
        P(),
        P(),
        P("ty", "tx", None, None, None),
        P("ty", "tx", None, None),
        P(),
    )
    return jax.shard_map(
        shards, mesh=mesh, in_specs=placed, out_specs=P(None, None, "ty", "tx"), check_vma=False
    )
```
